512 devices in a mesh: node: 128 (over z, y, core), local: 4 (over x).
Axes of the slice: x: 4, y: 4, z: 16, core: 2. Of those that a mesh axis runs over, the one named last changes fastest.
Arguments:
- table: bfloat16 [131072, 512], P(('node', 'local')), may hold values from -6 to 6
- w_in: bfloat16 [1, 512, 2048], replicated, may hold values from -0.25 to 0.25
- w_out: bfloat16 [1, 512, 512], replicated, may hold values from -0.25 to 0.25
- owner_node: int32 [131072, 1], P(('node', 'local')), may hold values from 0 to 127; in each aligned block of 256 rows (0 to 255, 256 to 511, ...) at most 3 rows name the same one
- item_row: int32 [131072], P(('node', 'local')), may hold values from 0 to 1023
- history_lengths: int32 [512, 4], P(('node', 'local')), may hold values from 1 to 128, 256 in all within a row
- cotangent: bfloat16 [131072, 512], P(('node', 'local')), may hold values from -6 to 6
Outputs:
- table_grad: bfloat16 [131072, 512], P(('node', 'local'))
The draws below stay inside these ranges and needn't reach their ends.
Inputs may be any that keep to these rules, and one draw needn't show every extreme that they name: `owner_node`: of the 256 items of one device, at most 3 name the same node, and this many do in some device's items in every draw. `history_lengths`: each row sums to 256, and some history is 128 items long.
All inputs are finite; a program needn't handle non-finite values.
Results may differ from the reference program's by a relative error of at most 0.018.
Values may be sent and summed in bfloat16 or wider, within the bound.
No kernel may reach another device: no remote copies, remote signals or barrier semaphores. Data moves between devices by JAX's collectives and lax.ppermute only.
A program may use at most 64 MiB of HBM per device.

```python
import math
import jax
import jax.numpy as jnp
import numpy as np
from jax import lax

D = 512
HEADS = 4
LAYERS = 1
TOK_DEV = 256
SEQS = 4
LONGEST = 128
CAP = 3
NODE_ROWS = 1024
VOCAB = 131072
TOKENS = 131072
N_NODE = 128
DEVICES = 512


def with_ends(result, stream_key, least, high):
    place = [jax.random.randint(jax.random.fold_in(stream_key, axis), (), 0, length) for axis, length in enumerate(result.shape)]
    widest = result.shape.index(max(result.shape))
    beside = place[:widest] + [(place[widest] + 1) % result.shape[widest]] + place[widest + 1:]
    return result.at[tuple(place)].set(least).at[tuple(beside)].set(high)


def block_levels(own_key, shape, cuts, low, largest):
    gain = 1.0
    for position, shards_of in cuts:
        draws = jax.random.uniform(jax.random.fold_in(jax.random.fold_in(own_key, 6), position), (shards_of,), jnp.float32, low / len(cuts), largest / len(cuts))
        gain = gain * jnp.repeat(jnp.exp(draws), shape[position] // shards_of).reshape((-1,) + (1,) * (len(shape) - 1 - position))
    return gain


def profile(count, total, bound, slope):
    weights = [(1 << 20) // math.isqrt(grade ** slope) + 1 for grade in range(2, count + 1)]
    spare, given = total - bound - (count - 1), [1] * (count - 1)
    while spare > 0:
        movable = [i for i in range(count - 1) if given[i] < bound]
        whole, remaining = sum([weights[i] for i in movable]), spare
        for i in movable:
            extra = min(bound - given[i], max(1, remaining * weights[i] // whole), spare)
            given[i] = given[i] + extra
            spare = spare - extra
    return np.array([bound] + given)


def ragged_sizes(key, amount, total, limit, lean):
    if amount == 2:
        one = jax.random.randint(key, (), max(1, total - limit), min(limit, total - 1) + 1)
        return jnp.stack([one, total - one])
    tallies = jnp.asarray(profile(amount, total, limit, lean), jnp.int32)
    couples = (amount - 1) // 2
    source_of, taker = tallies[1:1 + 2 * couples:2], tallies[2:2 + 2 * couples:2]
    slack = jnp.minimum(source_of - 1, limit - taker)
    passed = jax.random.randint(jax.random.fold_in(key, 1), (couples,), 0, 1 << 20) % (slack + 1)
    tallies = tallies.at[1:1 + 2 * couples:2].set(source_of - passed).at[2:2 + 2 * couples:2].set(taker + passed)
    return tallies[jax.random.permutation(jax.random.fold_in(key, 2), amount)]


def routed_block(key, own, number, rows, amount, top, most, slope):
    ranking = jax.random.permutation(key, amount)
    crowded, usual = portions_of(amount, rows * top, most, slope, True), portions_of(amount, rows * top, most, slope, False)
    places = jnp.arange(amount)

    def named(tallies, turn):
        used = int((tallies > 0).sum())
        fixed = max(1, used // 4)
        moved = fixed + (places - fixed + turn * (used - fixed)) % max(1, amount - fixed)
        return jnp.zeros((amount,), jnp.int32).at[ranking[jnp.where(places < fixed, places, moved)]].set(jnp.asarray(tallies, jnp.int32))

    tallies = jnp.where(number % 4 == 0, named(crowded, number // 4), named(usual, number - number // 4 - 1))
    mixed = jax.random.permutation(jax.random.fold_in(own, 3), amount)
    donor, sink = mixed[0:amount // 2 * 2:2], mixed[1:amount // 2 * 2:2]
    slack = jnp.minimum(tallies[donor] - 1, most - tallies[sink]) // 2
    slack = jnp.where((donor == ranking[0]) | (sink == ranking[0]) | (tallies[sink] == 0), 0, jnp.maximum(slack, 0))
    moved = jax.random.randint(jax.random.fold_in(own, 4), (amount // 2,), 0, 1 << 20) % (slack + 1)
    tallies = tallies.at[donor].add(-moved).at[sink].add(moved)
    labels = jnp.searchsorted(jnp.cumsum(tallies), jnp.arange(rows * top), side="right").astype(jnp.int32)
    listing = labels.reshape(top, rows).T
    listing = listing[jax.random.permutation(jax.random.fold_in(own, 1), rows)]
    turn = jax.random.randint(jax.random.fold_in(own, 2), (rows, 1), 0, top)
    return jnp.take_along_axis(listing, (jnp.arange(top)[None, :] + turn) % top, axis=1)


def portions_of(amount, total, most, slope, full):
    weights = [(1 << 20) // math.isqrt(standing ** slope) + 1 for standing in range(1, amount + 1)]
    largest = most if full else min(most, max(-(-total // amount), total * weights[0] // sum(weights)))
    least = 1 if total - largest >= amount - 1 else 0
    given, surplus = [largest] + [least] * (amount - 1), total - largest - least * (amount - 1)
    while surplus > 0:
        candidates = [i for i in range(1, amount) if given[i] < largest] or [i for i in range(1, amount) if given[i] < most]
        whole, remaining = sum([weights[i] for i in candidates]), surplus
        for i in candidates:
            extra = min(most - given[i], max(1, remaining * weights[i] // whole), surplus)
            given[i] = given[i] + extra
            surplus = surplus - extra
    return np.array(given)


def centred(own_key, extent, deviation, limit, shards=(), kind=jnp.bfloat16):
    gain = block_levels(own_key, extent, shards, -0.22, 0.18) if shards else 1.0
    values = jax.random.normal(own_key, extent, jnp.float32) * deviation * gain
    return jnp.minimum(jnp.maximum(values, -limit), limit).astype(kind)


def setup_inputs(seed: int = 0) -> dict:
    arg_keys = jax.random.split(jax.random.key(seed), 8)
    table = centred(arg_keys[0], (VOCAB, D), 1.0, 6.0, ((0, 512),))
    w_in = centred(arg_keys[1], (LAYERS, D, 4 * D), D ** -0.5, 0.25)
    w_out = centred(arg_keys[2], (LAYERS, D, D), D ** -0.5, 0.25)
    owner_node_keys = jax.random.split(jax.random.fold_in(arg_keys[3], 1), TOKENS // TOK_DEV)
    owner_node_turns = jax.random.permutation(jax.random.fold_in(arg_keys[3], 3), TOKENS // TOK_DEV)
    owner_node = jax.vmap(lambda own, number: routed_block(jax.random.fold_in(arg_keys[3], 2), own, number, TOK_DEV, N_NODE, 1, CAP, 2))(owner_node_keys, owner_node_turns).reshape((TOKENS, 1))
    item_row = with_ends(jax.random.randint(arg_keys[4], (TOKENS,), 0, NODE_ROWS), jax.random.fold_in(arg_keys[4], 1), 0, NODE_ROWS - 1).astype(jnp.int32)
    history_lengths = jax.vmap(lambda own: ragged_sizes(own, SEQS, TOK_DEV, LONGEST, 2))(jax.random.split(arg_keys[5], DEVICES)).reshape((DEVICES, SEQS)).astype(jnp.int32)
    cotangent = centred(arg_keys[6], (TOKENS, D), 1.0, 6.0, ((0, 512),))
    return {"table": table, "w_in": w_in, "w_out": w_out, "owner_node": owner_node, "item_row": item_row, "history_lengths": history_lengths, "cotangent": cotangent}


def normalize(value):
    average = lax.optimization_barrier(jnp.mean(value, axis=-1, keepdims=True))
    centered = value - average
    spread = lax.optimization_barrier(jnp.mean(centered * centered, axis=-1, keepdims=True))
    return centered * lax.rsqrt(spread + 1e-05)

def history_weights(lengths, tok_rows):
    seq_ends = jnp.cumsum(lengths).astype(jnp.int32)
    places = jnp.arange(tok_rows, dtype=jnp.int32)
    segment = lax.optimization_barrier(jnp.sum((places[:, None] >= seq_ends[None, :]).astype(jnp.int32), axis=1))
    member = segment[:, None] == jnp.arange(lengths.shape[0], dtype=jnp.int32)[None, :]
    own_length = lax.optimization_barrier(jnp.sum(jnp.where(member, lengths[None, :], 0), axis=1))
    allowed = (segment[:, None] == segment[None, :]) & (places[None, :] <= places[:, None])
    factor = 1.0 / own_length.astype(jnp.float32)
    return jnp.where(allowed, factor[:, None], jnp.float32(0.0)).astype(jnp.float32)

def one_layer(hidden, weights, layer_in, layer_out):
    tok_rows = hidden.shape[0]
    model_width = hidden.shape[1]
    head_size = model_width // HEADS
    normed = normalize(hidden).astype(jnp.bfloat16)
    projected = jax.nn.silu(jnp.dot(normed, layer_in, preferred_element_type=jnp.float32)).astype(jnp.bfloat16)
    gate_rows = projected[:, :model_width]
    value_rows = projected[:, model_width:2 * model_width]
    query_rows = projected[:, 2 * model_width:3 * model_width]
    key_rows = projected[:, 3 * model_width:]

    def by_head(part):
        return part.reshape(tok_rows, HEADS, head_size).transpose(1, 0, 2)
    scale = 1.0 / math.sqrt(head_size)

    def one_head(head_parts):
        query_head, key_head, value_head = head_parts
        scores = jnp.dot(query_head, key_head.T, preferred_element_type=jnp.float32) * scale
        attention = (jax.nn.silu(scores) * weights).astype(jnp.bfloat16)
        return jnp.dot(attention, value_head, preferred_element_type=jnp.float32)
    mixed_rows = lax.map(jax.checkpoint(one_head), (by_head(query_rows), by_head(key_rows), by_head(value_rows)))
    mixed_rows = mixed_rows.transpose(1, 0, 2).reshape(tok_rows, model_width)
    gated_rows = (normalize(mixed_rows) * gate_rows.astype(jnp.float32)).astype(jnp.bfloat16)
    return jnp.dot(gated_rows, layer_out, preferred_element_type=jnp.float32) + hidden

def layer_stack(embedded, weights, w_in, w_out):
    hidden = embedded.astype(jnp.float32)
    for layer_index in range(w_in.shape[0]):
        hidden = one_layer(hidden, weights, w_in[layer_index], w_out[layer_index])
    return hidden

def embedding_grad(embedded, lengths, cot_rows, w_in, w_out):
    weights = history_weights(lengths, embedded.shape[0])
    outputs, pullback = jax.vjp(lambda entries: layer_stack(entries, weights, w_in, w_out), embedded)
    return pullback(cot_rows.astype(outputs.dtype))[0]

def reference(table, w_in, w_out, owner_node, item_row, history_lengths, cotangent):
    table_rows = (owner_node[:, 0] * NODE_ROWS + item_row).astype(jnp.int32).reshape(DEVICES, TOK_DEV)
    cot_blocks = cotangent.reshape(DEVICES, TOK_DEV, D)

    def accumulate(row_totals, inputs):
        rows_here, lengths_here, cot_here = inputs
        embedded = table[rows_here]
        grads = embedding_grad(embedded, lengths_here, cot_here, w_in, w_out)
        return (row_totals.at[rows_here].add(grads.astype(jnp.float32)), None)
    start = jnp.zeros((VOCAB, D), jnp.float32)
    row_totals, unused = lax.scan(accumulate, start, (table_rows, history_lengths, cot_blocks))
    return row_totals.astype(jnp.bfloat16)
```

```python
import math

import jax
import jax.numpy as jnp
from jax import lax
from jax.experimental import pallas as pl
from jax.experimental.pallas import tpu as pltpu
from jax.sharding import PartitionSpec as P

HEADS = 4
CAP = 3
LANES = 128
F32 = jnp.float32
BF16 = jnp.bfloat16
VMEM = pl.BlockSpec(memory_space=pltpu.VMEM)
SMEM = pl.BlockSpec(memory_space=pltpu.SMEM)


def dot(a, b, ca=1, cb=0):
    return lax.dot_general(a, b, (((ca,), (cb,)), ((), ())), preferred_element_type=F32)


def ranked(owner, nodes):
    count = owner.shape[0]
    hot = owner == lax.broadcasted_iota(jnp.int32, (count, nodes), 1)
    hot = jnp.where(hot, 1.0, 0.0)
    row = lax.broadcasted_iota(jnp.int32, (count, count), 0)
    col = lax.broadcasted_iota(jnp.int32, (count, count), 1)
    earlier = jnp.where(col < row, 1.0, 0.0).astype(BF16)
    before = dot(earlier, hot.astype(BF16))
    rank = jnp.sum(before * hot, axis=1, keepdims=True)
    return hot, rank


def ask_kernel(owner_ref, row_ref, ids_ref):
    nodes = ids_ref.shape[0]
    count = owner_ref.shape[0]
    hot, rank = ranked(owner_ref[...], nodes)
    rows = row_ref[...]
    place = lax.broadcasted_iota(jnp.int32, (count, LANES), 1) == rank.astype(jnp.int32)
    high = jnp.where(place, (rows >> 5).astype(F32), 0.0).astype(BF16)
    low = jnp.where(place, (rows & 31).astype(F32), 0.0).astype(BF16)
    hot = hot.astype(BF16)
    ids = dot(hot, high, 0, 0) * 32.0 + dot(hot, low, 0, 0)
    ids_ref[...] = ids.astype(jnp.int32)


def answer_kernel(ids_ref, table_ref, out_ref, wide_ref):
    nodes = ids_ref.shape[0]
    rows, width = table_ref.shape
    pieces = width // LANES
    ids = ids_ref[...]
    table = table_ref[...]
    place = lax.broadcasted_iota(jnp.int32, (nodes, rows), 1)
    for slot in range(CAP):
        hot = jnp.where(ids[:, slot : slot + 1] == place, 1.0, 0.0).astype(BF16)
        picked = dot(hot, table)
        for piece in range(pieces):
            wide_ref[pl.ds(slot * pieces + piece, nodes, stride=CAP * pieces), :] = picked[
                :, piece * LANES : (piece + 1) * LANES
            ]
    out_ref[...] = wide_ref[...].astype(BF16)


def unpack(message_ref, wide_ref, nodes, pieces):
    wide_ref[...] = message_ref[...].astype(F32)
    slots = []
    for slot in range(CAP):
        parts = [
            wide_ref[pl.ds(slot * pieces + piece, nodes, stride=CAP * pieces), :].astype(BF16)
            for piece in range(pieces)
        ]
        slots.append(jnp.concatenate(parts, axis=1))
    return slots


def centre(value):
    average = jnp.mean(value, axis=1, keepdims=True)
    centered = value - average
    spread = jnp.mean(centered * centered, axis=1, keepdims=True)
    inverse = lax.rsqrt(spread + 1e-05)
    return centered * inverse, inverse


def centre_back(normed, inverse, cot):
    return inverse * (
        cot
        - jnp.mean(cot, axis=1, keepdims=True)
        - normed * jnp.mean(cot * normed, axis=1, keepdims=True)
    )


def gated(value):
    gate = 0.5 + 0.5 * jnp.tanh(0.5 * value)
    kept = value * gate
    return kept, gate + kept * (1.0 - gate)


def layer_kernel(lengths_ref, owner_ref, message_ref, cot_ref, w_in_ref, w_out_ref, out_ref, wide_ref):
    tokens, width = cot_ref.shape
    head = width // HEADS
    pieces = width // LANES
    nodes = message_ref.shape[0] // (CAP * pieces)
    hot, rank = ranked(owner_ref[...], nodes)
    picks = [jnp.where(rank == float(slot), hot, 0.0).astype(BF16) for slot in range(CAP)]
    arrived = unpack(message_ref, wide_ref, nodes, pieces)
    embedded = dot(jnp.concatenate(picks, axis=1), jnp.concatenate(arrived, axis=0))

    row = lax.broadcasted_iota(jnp.int32, (tokens, 1), 0)
    col = lax.broadcasted_iota(jnp.int32, (1, tokens), 1)
    seqs = lengths_ref.shape[1]
    row_seg, col_seg, end = jnp.zeros_like(row), jnp.zeros_like(col), jnp.int32(0)
    own = jnp.full((tokens, 1), lengths_ref[0, 0], jnp.int32)
    for seq in range(seqs - 1):
        end = end + lengths_ref[0, seq]
        row_seg = row_seg + (row >= end).astype(jnp.int32)
        col_seg = col_seg + (col >= end).astype(jnp.int32)
        own = jnp.where(row >= end, lengths_ref[0, seq + 1], own)
    factor = 1.0 / own.astype(F32)
    weights = jnp.where((row_seg == col_seg) & (col <= row), factor, 0.0)

    normed, inverse = centre(embedded)
    normed_low = normed.astype(BF16)
    parts, slopes = [], []
    for part in range(4):
        kept, slope = gated(dot(normed_low, w_in_ref[:, part * width : (part + 1) * width]))
        parts.append(kept.astype(BF16))
        slopes.append(slope)
    gate_rows, value_rows, query_rows, key_rows = parts
    scale = 1.0 / math.sqrt(head)
    attentions, score_slopes, mixed = [], [], []
    for e in range(HEADS):
        cols = slice(e * head, (e + 1) * head)
        kept, slope = gated(dot(query_rows[:, cols], key_rows[:, cols], 1, 1) * scale)
        attention = (kept * weights).astype(BF16)
        attentions.append(attention)
        score_slopes.append(slope * (weights * scale))
        mixed.append(dot(attention, value_rows[:, cols]))
    mixed_normed, mixed_inverse = centre(jnp.concatenate(mixed, axis=1))

    cot = cot_ref[...]
    gated_cot = dot(cot, w_out_ref[...], 1, 1).astype(BF16).astype(F32)
    gate_cot = gated_cot * mixed_normed
    mixed_cot = centre_back(mixed_normed, mixed_inverse, gated_cot * gate_rows.astype(F32)).astype(BF16)
    value_cots, query_cots, key_cots = [], [], []
    for e in range(HEADS):
        cols = slice(e * head, (e + 1) * head)
        head_cot = mixed_cot[:, cols]
        value_cots.append(dot(attentions[e], head_cot, 0, 0))
        score_cot = (dot(head_cot, value_rows[:, cols], 1, 1) * score_slopes[e]).astype(BF16)
        query_cots.append(dot(score_cot, key_rows[:, cols]))
        key_cots.append(dot(score_cot, query_rows[:, cols], 0, 0))
    normed_cot = jnp.zeros((tokens, width), F32)
    for part, part_cot in enumerate([[gate_cot], value_cots, query_cots, key_cots]):
        whole = part_cot[0] if len(part_cot) == 1 else jnp.concatenate(part_cot, axis=1)
        whole = (whole.astype(BF16).astype(F32) * slopes[part]).astype(BF16)
        normed_cot = normed_cot + dot(whole, w_in_ref[:, part * width : (part + 1) * width], 1, 1)
    grads = cot.astype(F32) + centre_back(normed, inverse, normed_cot.astype(BF16).astype(F32))
    grads = grads.astype(BF16)
    for slot in range(CAP):
        placed = dot(picks[slot], grads, 0, 0)
        for piece in range(pieces):
            wide_ref[pl.ds(slot * pieces + piece, nodes, stride=CAP * pieces), :] = placed[
                :, piece * LANES : (piece + 1) * LANES
            ]
    out_ref[...] = wide_ref[...].astype(BF16)


def total_kernel(ids_ref, message_ref, out_ref, wide_ref):
    nodes = ids_ref.shape[0]
    rows, width = out_ref.shape
    arrived = unpack(message_ref, wide_ref, nodes, width // LANES)
    ids = ids_ref[...]
    place = lax.broadcasted_iota(jnp.int32, (nodes, rows), 1)
    total = jnp.zeros((rows, width), F32)
    for slot in range(CAP):
        hot = jnp.where(ids[:, slot : slot + 1] == place, 1.0, 0.0).astype(BF16)
        total = total + dot(hot, arrived[slot], 0, 0)
    out_ref[...] = total.astype(BF16)


def kernel_call(body, out_shape, out_type, ins, wide=0, limit=32):
    return pl.pallas_call(
        body,
        out_shape=jax.ShapeDtypeStruct(out_shape, out_type),
        in_specs=ins,
        out_specs=VMEM,
        scratch_shapes=[pltpu.VMEM((wide, LANES), F32)] if wide else [],
        compiler_params=pltpu.CompilerParams(vmem_limit_bytes=limit << 20),
    )


def per_device(table, w_in, w_out, owner_node, item_row, history_lengths, cotangent):
    tokens = item_row.shape[0]
    nodes = lax.axis_size("node")
    locals_ = lax.axis_size("local")
    rows_here, width = table.shape
    pieces = width // LANES
    wide = nodes * CAP * pieces

    def exchange(message):
        message = message.reshape(nodes, CAP, pieces, LANES)
        message = lax.all_to_all(message, "node", split_axis=0, concat_axis=0, tiled=True)
        return message.reshape(wide, LANES)

    node_rows = lax.all_gather(table, "local", axis=0, tiled=True)
    sent = kernel_call(ask_kernel, (nodes, LANES), jnp.int32, [VMEM, VMEM])(
        owner_node, item_row.reshape(tokens, 1)
    )
    asked = lax.all_to_all(sent, "node", split_axis=0, concat_axis=0, tiled=True)
    answers = kernel_call(answer_kernel, (wide, LANES), BF16, [VMEM, VMEM], wide)(asked, node_rows)
    arrived = exchange(answers)
    grads = kernel_call(layer_kernel, (wide, LANES), BF16, [SMEM] + [VMEM] * 5, wide, 56)(
        history_lengths, owner_node, arrived, cotangent, w_in[0], w_out[0]
    )
    node_grads = exchange(grads)
    totals = kernel_call(total_kernel, (locals_ * rows_here, width), BF16, [VMEM, VMEM], wide)(
        asked, node_grads
    )
    totals = lax.all_to_all(
        totals.reshape(locals_, rows_here, width), "local", split_axis=0, concat_axis=0, tiled=True
    )
    return jnp.sum(totals.astype(F32), axis=0).astype(BF16)


def solution(mesh):
    return jax.shard_map(
        per_device,
        mesh=mesh,
        in_specs=(
            P(("node", "local"), None),
            P(),
            P(),
            P(("node", "local"), None),
            P(("node", "local")),
            P(("node", "local"), None),
            P(("node", "local"), None),
        ),
        out_specs=P(("node", "local"), None),
        check_vma=False,
    )
```

```python
import math

import jax
import jax.numpy as jnp
from jax import lax
from jax.experimental import pallas as pl
from jax.experimental.pallas import tpu as pltpu
from jax.sharding import PartitionSpec as P

HEADS = 4
CAP = 3
LANES = 128
F32 = jnp.float32
BF16 = jnp.bfloat16
VMEM = pl.BlockSpec(memory_space=pltpu.VMEM)
SMEM = pl.BlockSpec(memory_space=pltpu.SMEM)


def dot(a, b, ca=1, cb=0):
    return lax.dot_general(a, b, (((ca,), (cb,)), ((), ())), preferred_element_type=F32)


def ranked(owner, nodes):
    count = owner.shape[1]
    hot = jnp.where(owner == lax.broadcasted_iota(jnp.int32, (nodes, count), 0), 1.0, 0.0)
    row = lax.broadcasted_iota(jnp.int32, (count, count), 0)
    col = lax.broadcasted_iota(jnp.int32, (count, count), 1)
    earlier = jnp.where(row < col, 1.0, 0.0).astype(BF16)
    before = dot(hot.astype(BF16), earlier)
    return hot, jnp.sum(before * hot, axis=0, keepdims=True)


def ask_kernel(owner_ref, row_ref, ids_ref):
    nodes, lanes = ids_ref.shape
    count = owner_ref.shape[1]
    hot, rank = ranked(owner_ref[...], nodes)
    rows = row_ref[...]
    place = lax.broadcasted_iota(jnp.int32, (lanes, count), 0) == rank.astype(jnp.int32)
    high = jnp.where(place, (rows >> 5).astype(F32), 0.0).astype(BF16)
    low = jnp.where(place, (rows & 31).astype(F32), 0.0).astype(BF16)
    hot = hot.astype(BF16)
    ids = dot(hot, high, 1, 1) * 32.0 + dot(hot, low, 1, 1)
    ids_ref[...] = ids.astype(jnp.int32)


def answer_kernel(place_ref, ids_ref, *refs):
    blocks, out_ref, wide_ref = refs[:-2], refs[-2], refs[-1]
    nodes = ids_ref.shape[0]
    rows, width = blocks[0].shape
    pieces = width // LANES
    ids = ids_ref[...] - place_ref[0] * rows
    ids = jnp.where(ids < 0, ids + len(blocks) * rows, ids)
    at = lax.broadcasted_iota(jnp.int32, (nodes, rows), 1)
    tables = [block[...] for block in blocks]
    for slot in range(CAP):
        picked = jnp.zeros((nodes, width), F32)
        for turn, table in enumerate(tables):
            hot = jnp.where(ids[:, slot : slot + 1] - turn * rows == at, 1.0, 0.0).astype(BF16)
            picked = picked + dot(hot, table)
        spread(picked, slot, wide_ref, nodes, pieces)
    out_ref[...] = wide_ref[...].astype(BF16)


def spread(value, slot, wide_ref, nodes, pieces):
    for piece in range(pieces):
        wide_ref[pl.ds(slot * pieces + piece, nodes, stride=CAP * pieces), :] = value[
            :, piece * LANES : (piece + 1) * LANES
        ]


def unpack(message_ref, wide_ref, nodes, pieces):
    wide_ref[...] = message_ref[...].astype(F32)
    slots = []
    for slot in range(CAP):
        parts = [
            wide_ref[pl.ds(slot * pieces + piece, nodes, stride=CAP * pieces), :].astype(BF16)
            for piece in range(pieces)
        ]
        slots.append(jnp.concatenate(parts, axis=1))
    return slots


def centre(value):
    average = jnp.mean(value, axis=1, keepdims=True)
    centered = value - average
    spread = jnp.mean(centered * centered, axis=1, keepdims=True)
    inverse = lax.rsqrt(spread + 1e-05)
    return centered * inverse, inverse


def centre_back(normed, inverse, cot):
    return inverse * (
        cot
        - jnp.mean(cot, axis=1, keepdims=True)
        - normed * jnp.mean(cot * normed, axis=1, keepdims=True)
    )


def gated(value):
    gate = 0.5 + 0.5 * jnp.tanh(0.5 * value)
    kept = value * gate
    return kept, gate + kept * (1.0 - gate)


def layer_kernel(lengths_ref, owner_ref, message_ref, cot_ref, w_in_ref, w_out_ref, out_ref, wide_ref):
    tokens, width = cot_ref.shape
    head = width // HEADS
    pieces = width // LANES
    nodes = message_ref.shape[0] // (CAP * pieces)
    hot, rank = ranked(owner_ref[...], nodes)
    picks = [jnp.where(rank == float(slot), hot, 0.0).astype(BF16) for slot in range(CAP)]
    arrived = unpack(message_ref, wide_ref, nodes, pieces)
    embedded = dot(jnp.concatenate(picks, axis=0), jnp.concatenate(arrived, axis=0), 0, 0)

    row = lax.broadcasted_iota(jnp.int32, (tokens, 1), 0)
    col = lax.broadcasted_iota(jnp.int32, (1, tokens), 1)
    seqs = lengths_ref.shape[1]
    row_seg, col_seg, end = jnp.zeros_like(row), jnp.zeros_like(col), jnp.int32(0)
    own = jnp.full((tokens, 1), lengths_ref[0, 0], jnp.int32)
    for seq in range(seqs - 1):
        end = end + lengths_ref[0, seq]
        row_seg = row_seg + (row >= end).astype(jnp.int32)
        col_seg = col_seg + (col >= end).astype(jnp.int32)
        own = jnp.where(row >= end, lengths_ref[0, seq + 1], own)
    factor = 1.0 / own.astype(F32)
    weights = jnp.where((row_seg == col_seg) & (col <= row), factor, 0.0)

    normed, inverse = centre(embedded)
    normed_low = normed.astype(BF16)
    parts, slopes = [], []
    for part in range(4):
        kept, slope = gated(dot(normed_low, w_in_ref[:, part * width : (part + 1) * width]))
        parts.append(kept.astype(BF16))
        slopes.append(slope)
    gate_rows, value_rows, query_rows, key_rows = parts
    scale = 1.0 / math.sqrt(head)
    attentions, score_slopes, mixed = [], [], []
    for e in range(HEADS):
        cols = slice(e * head, (e + 1) * head)
        kept, slope = gated(dot(query_rows[:, cols], key_rows[:, cols], 1, 1) * scale)
        attention = (kept * weights).astype(BF16)
        attentions.append(attention)
        score_slopes.append(slope * (weights * scale))
        mixed.append(dot(attention, value_rows[:, cols]))
    mixed_normed, mixed_inverse = centre(jnp.concatenate(mixed, axis=1))

    cot = cot_ref[...]
    gated_cot = dot(cot, w_out_ref[...], 1, 1).astype(BF16).astype(F32)
    gate_cot = gated_cot * mixed_normed
    mixed_cot = centre_back(mixed_normed, mixed_inverse, gated_cot * gate_rows.astype(F32)).astype(BF16)
    value_cots, query_cots, key_cots = [], [], []
    for e in range(HEADS):
        cols = slice(e * head, (e + 1) * head)
        head_cot = mixed_cot[:, cols]
        value_cots.append(dot(attentions[e], head_cot, 0, 0))
        score_cot = (dot(head_cot, value_rows[:, cols], 1, 1) * score_slopes[e]).astype(BF16)
        query_cots.append(dot(score_cot, key_rows[:, cols]))
        key_cots.append(dot(score_cot, query_rows[:, cols], 0, 0))
    normed_cot = jnp.zeros((tokens, width), F32)
    for part, part_cot in enumerate([[gate_cot], value_cots, query_cots, key_cots]):
        whole = part_cot[0] if len(part_cot) == 1 else jnp.concatenate(part_cot, axis=1)
        whole = (whole.astype(BF16).astype(F32) * slopes[part]).astype(BF16)
        normed_cot = normed_cot + dot(whole, w_in_ref[:, part * width : (part + 1) * width], 1, 1)
    grads = cot.astype(F32) + centre_back(normed, inverse, normed_cot.astype(BF16).astype(F32))
    grads = grads.astype(BF16)
    for slot in range(CAP):
        spread(dot(picks[slot], grads), slot, wide_ref, nodes, pieces)
    out_ref[...] = wide_ref[...].astype(BF16)


def total_kernel(ids_ref, message_ref, out_ref, wide_ref):
    nodes = ids_ref.shape[0]
    rows, width = out_ref.shape
    arrived = unpack(message_ref, wide_ref, nodes, width // LANES)
    ids = ids_ref[...]
    place = lax.broadcasted_iota(jnp.int32, (nodes, rows), 1)
    total = jnp.zeros((rows, width), F32)
    for slot in range(CAP):
        hot = jnp.where(ids[:, slot : slot + 1] == place, 1.0, 0.0).astype(BF16)
        total = total + dot(hot, arrived[slot], 0, 0)
    out_ref[...] = total.astype(BF16)


def sum_kernel(parts_ref, out_ref):
    total = parts_ref[0].astype(F32)
    for part in range(1, parts_ref.shape[0]):
        total = total + parts_ref[part].astype(F32)
    out_ref[...] = total.astype(BF16)


def kernel_call(body, out_shape, out_type, ins, wide=0, limit=32):
    return pl.pallas_call(
        body,
        out_shape=jax.ShapeDtypeStruct(out_shape, out_type),
        in_specs=ins,
        out_specs=VMEM,
        scratch_shapes=[pltpu.VMEM((wide, LANES), F32)] if wide else [],
        compiler_params=pltpu.CompilerParams(vmem_limit_bytes=limit << 20),
    )


def per_device(table, w_in, w_out, owner_node, item_row, history_lengths, cotangent):
    tokens = item_row.shape[0]
    nodes = lax.axis_size("node")
    locals_ = lax.axis_size("local")
    rows_here, width = table.shape
    pieces = width // LANES
    wide = nodes * CAP * pieces

    def exchange(message):
        message = message.reshape(nodes, CAP, pieces, LANES)
        message = lax.all_to_all(message, "node", split_axis=0, concat_axis=0, tiled=True)
        return message.reshape(wide, LANES)

    def turned(block, by):
        return lax.ppermute(block, "local", [((i + by) % locals_, i) for i in range(locals_)])

    blocks = [table] + [turned(table, by) for by in range(1, locals_)]
    owner = owner_node.reshape(1, tokens)
    sent = kernel_call(ask_kernel, (nodes, LANES), jnp.int32, [VMEM, VMEM])(
        owner, item_row.reshape(1, tokens)
    )
    asked = lax.all_to_all(sent, "node", split_axis=0, concat_axis=0, tiled=True)
    place = lax.axis_index("local").reshape(1)
    answers = kernel_call(
        answer_kernel, (wide, LANES), BF16, [SMEM, VMEM] + [VMEM] * locals_, wide
    )(place, asked, *blocks)
    arrived = exchange(answers)
    grads = kernel_call(layer_kernel, (wide, LANES), BF16, [SMEM] + [VMEM] * 5, wide, 56)(
        history_lengths, owner, arrived, cotangent, w_in[0], w_out[0]
    )
    node_grads = exchange(grads)
    totals = kernel_call(total_kernel, (locals_ * rows_here, width), BF16, [VMEM, VMEM], wide)(
        asked, node_grads
    )
    totals = lax.all_to_all(
        totals.reshape(locals_, rows_here, width), "local", split_axis=0, concat_axis=0, tiled=True
    )
    return kernel_call(sum_kernel, (rows_here, width), BF16, [VMEM])(totals)


def solution(mesh):
    return jax.shard_map(
        per_device,
        mesh=mesh,
        in_specs=(
            P(("node", "local"), None),
            P(),
            P(),
            P(("node", "local"), None),
            P(("node", "local")),
            P(("node", "local"), None),
            P(("node", "local"), None),
        ),
        out_specs=P(("node", "local"), None),
        check_vma=False,
    )
```

```python
import math

import jax
import jax.numpy as jnp
from jax import lax
from jax.experimental import pallas as pl
from jax.experimental.pallas import tpu as pltpu
from jax.sharding import PartitionSpec as P

HEADS = 4
CAP = 3
LANES = 128
F32 = jnp.float32
BF16 = jnp.bfloat16
VMEM = pl.BlockSpec(memory_space=pltpu.VMEM)
SMEM = pl.BlockSpec(memory_space=pltpu.SMEM)


def dot(a, b, ca=1, cb=0):
    return lax.dot_general(a, b, (((ca,), (cb,)), ((), ())), preferred_element_type=F32)


def ranked(owner, nodes):
    count = owner.shape[1]
    hot = jnp.where(owner == lax.broadcasted_iota(jnp.int32, (nodes, count), 0), 1.0, 0.0)
    row = lax.broadcasted_iota(jnp.int32, (count, count), 0)
    col = lax.broadcasted_iota(jnp.int32, (count, count), 1)
    earlier = jnp.where(row < col, 1.0, 0.0).astype(BF16)
    before = dot(hot.astype(BF16), earlier)
    return hot, jnp.sum(before * hot, axis=0, keepdims=True)


def ask_kernel(owner_ref, row_ref, ids_ref):
    nodes, lanes = ids_ref.shape
    count = owner_ref.shape[1]
    hot, rank = ranked(owner_ref[...], nodes)
    rows = row_ref[...]
    place = lax.broadcasted_iota(jnp.int32, (lanes, count), 0) == rank.astype(jnp.int32)
    high = jnp.where(place, (rows >> 5).astype(F32), 0.0).astype(BF16)
    low = jnp.where(place, (rows & 31).astype(F32), 0.0).astype(BF16)
    hot = hot.astype(BF16)
    ids = dot(hot, high, 1, 1) * 32.0 + dot(hot, low, 1, 1)
    ids_ref[...] = ids.astype(jnp.int32)


def answer_kernel(place_ref, ids_ref, *refs):
    blocks, out_ref, wide_ref = refs[:-2], refs[-2], refs[-1]
    nodes = ids_ref.shape[0]
    rows, width = blocks[0].shape
    pieces = width // LANES
    ids = ids_ref[...] - place_ref[0] * rows
    ids = jnp.where(ids < 0, ids + len(blocks) * rows, ids)
    at = lax.broadcasted_iota(jnp.int32, (nodes, rows), 1)
    tables = [block[...] for block in blocks]
    for slot in range(CAP):
        picked = jnp.zeros((nodes, width), F32)
        for turn, table in enumerate(tables):
            hot = jnp.where(ids[:, slot : slot + 1] - turn * rows == at, 1.0, 0.0).astype(BF16)
            picked = picked + dot(hot, table)
        spread(picked, slot, wide_ref, nodes, pieces)
    out_ref[...] = wide_ref[...].astype(BF16)


def spread(value, slot, wide_ref, nodes, pieces):
    for piece in range(pieces):
        wide_ref[pl.ds(slot * pieces + piece, nodes, stride=CAP * pieces), :] = value[
            :, piece * LANES : (piece + 1) * LANES
        ]


def unpack(message_ref, wide_ref, nodes, pieces):
    wide_ref[...] = message_ref[...].astype(F32)
    slots = []
    for slot in range(CAP):
        parts = [
            wide_ref[pl.ds(slot * pieces + piece, nodes, stride=CAP * pieces), :].astype(BF16)
            for piece in range(pieces)
        ]
        slots.append(jnp.concatenate(parts, axis=1))
    return slots


def centre(value):
    average = jnp.mean(value, axis=1, keepdims=True)
    centered = value - average
    spread = jnp.mean(centered * centered, axis=1, keepdims=True)
    inverse = lax.rsqrt(spread + 1e-05)
    return centered * inverse, inverse


def centre_back(normed, inverse, cot):
    return inverse * (
        cot
        - jnp.mean(cot, axis=1, keepdims=True)
        - normed * jnp.mean(cot * normed, axis=1, keepdims=True)
    )


def gated(value):
    gate = 0.5 + 0.5 * jnp.tanh(0.5 * value)
    kept = value * gate
    return kept, gate + kept * (1.0 - gate)


def layer_kernel(lengths_ref, owner_ref, message_ref, cot_ref, w_in_ref, w_out_ref, out_ref, wide_ref):
    tokens, width = cot_ref.shape
    head = width // HEADS
    pieces = width // LANES
    nodes = message_ref.shape[0] // (CAP * pieces)
    hot, rank = ranked(owner_ref[...], nodes)
    picks = [jnp.where(rank == float(slot), hot, 0.0).astype(BF16) for slot in range(CAP)]
    arrived = unpack(message_ref, wide_ref, nodes, pieces)
    embedded = dot(jnp.concatenate(picks, axis=0), jnp.concatenate(arrived, axis=0), 0, 0)

    row = lax.broadcasted_iota(jnp.int32, (tokens, 1), 0)
    col = lax.broadcasted_iota(jnp.int32, (1, tokens), 1)
    seqs = lengths_ref.shape[1]
    row_seg, col_seg, end = jnp.zeros_like(row), jnp.zeros_like(col), jnp.int32(0)
    own = jnp.full((tokens, 1), lengths_ref[0, 0], jnp.int32)
    for seq in range(seqs - 1):
        end = end + lengths_ref[0, seq]
        row_seg = row_seg + (row >= end).astype(jnp.int32)
        col_seg = col_seg + (col >= end).astype(jnp.int32)
        own = jnp.where(row >= end, lengths_ref[0, seq + 1], own)
    factor = 1.0 / own.astype(F32)
    weights = jnp.where((row_seg == col_seg) & (col <= row), factor, 0.0)

    normed, inverse = centre(embedded)
    normed_low = normed.astype(BF16)
    parts, slopes = [], []
    for part in range(4):
        kept, slope = gated(dot(normed_low, w_in_ref[:, part * width : (part + 1) * width]))
        parts.append(kept.astype(BF16))
        slopes.append(slope)
    gate_rows, value_rows, query_rows, key_rows = parts
    scale = 1.0 / math.sqrt(head)
    weights = weights * scale
    attentions, score_slopes, mixed = [], [], []
    for e in range(HEADS):
        cols = slice(e * head, (e + 1) * head)
        scores = dot(query_rows[:, cols], key_rows[:, cols], 1, 1)
        gate = 0.5 + 0.5 * jnp.tanh((0.5 * scale) * scores)
        kept = scores * gate * weights
        score_slopes.append(weights * gate + kept * (scale - scale * gate))
        attentions.append(kept.astype(BF16))
        mixed.append(dot(attentions[e], value_rows[:, cols]))
    mixed_normed, mixed_inverse = centre(jnp.concatenate(mixed, axis=1))

    cot = cot_ref[...]
    gated_cot = dot(cot, w_out_ref[...], 1, 1).astype(BF16).astype(F32)
    gate_cot = gated_cot * mixed_normed
    mixed_cot = centre_back(mixed_normed, mixed_inverse, gated_cot * gate_rows.astype(F32)).astype(BF16)
    value_cots, query_cots, key_cots = [], [], []
    for e in range(HEADS):
        cols = slice(e * head, (e + 1) * head)
        head_cot = mixed_cot[:, cols]
        value_cots.append(dot(attentions[e], head_cot, 0, 0))
        score_cot = (dot(head_cot, value_rows[:, cols], 1, 1) * score_slopes[e]).astype(BF16)
        query_cots.append(dot(score_cot, key_rows[:, cols]))
        key_cots.append(dot(score_cot, query_rows[:, cols], 0, 0))
    normed_cot = jnp.zeros((tokens, width), F32)
    for part, part_cot in enumerate([[gate_cot], value_cots, query_cots, key_cots]):
        whole = part_cot[0] if len(part_cot) == 1 else jnp.concatenate(part_cot, axis=1)
        whole = (whole.astype(BF16).astype(F32) * slopes[part]).astype(BF16)
        normed_cot = normed_cot + dot(whole, w_in_ref[:, part * width : (part + 1) * width], 1, 1)
    grads = cot.astype(F32) + centre_back(normed, inverse, normed_cot.astype(BF16).astype(F32))
    grads = grads.astype(BF16)
    for slot in range(CAP):
        spread(dot(picks[slot], grads), slot, wide_ref, nodes, pieces)
    out_ref[...] = wide_ref[...].astype(BF16)


def total_kernel(ids_ref, message_ref, out_ref, wide_ref):
    nodes = ids_ref.shape[0]
    rows, width = out_ref.shape
    arrived = unpack(message_ref, wide_ref, nodes, width // LANES)
    ids = ids_ref[...]
    place = lax.broadcasted_iota(jnp.int32, (nodes, rows), 1)
    total = jnp.zeros((rows, width), F32)
    for slot in range(CAP):
        hot = jnp.where(ids[:, slot : slot + 1] == place, 1.0, 0.0).astype(BF16)
        total = total + dot(hot, arrived[slot], 0, 0)
    out_ref[...] = total.astype(BF16)


def sum_kernel(parts_ref, out_ref):
    total = parts_ref[0].astype(F32)
    for part in range(1, parts_ref.shape[0]):
        total = total + parts_ref[part].astype(F32)
    out_ref[...] = total.astype(BF16)


def kernel_call(body, out_shape, out_type, ins, wide=0, limit=32):
    return pl.pallas_call(
        body,
        out_shape=jax.ShapeDtypeStruct(out_shape, out_type),
        in_specs=ins,
        out_specs=VMEM,
        scratch_shapes=[pltpu.VMEM((wide, LANES), F32)] if wide else [],
        compiler_params=pltpu.CompilerParams(vmem_limit_bytes=limit << 20),
    )


def layer_call(wide, limit=24):
    return kernel_call(layer_kernel, (wide, LANES), BF16, [SMEM] + [VMEM] * 5, wide, limit)


def per_device(table, w_in, w_out, owner_node, item_row, history_lengths, cotangent):
    tokens = item_row.shape[0]
    nodes = lax.axis_size("node")
    locals_ = lax.axis_size("local")
    rows_here, width = table.shape
    pieces = width // LANES
    wide = nodes * CAP * pieces

    def exchange(message):
        message = message.reshape(nodes, CAP, pieces, LANES)
        message = lax.all_to_all(message, "node", split_axis=0, concat_axis=0, tiled=True)
        return message.reshape(wide, LANES)

    def turned(block, by):
        return lax.ppermute(block, "local", [((i + by) % locals_, i) for i in range(locals_)])

    blocks = [table] + [turned(table, by) for by in range(1, locals_)]
    owner = owner_node.reshape(1, tokens)
    sent = kernel_call(ask_kernel, (nodes, LANES), jnp.int32, [VMEM, VMEM], limit=60)(
        owner, item_row.reshape(1, tokens)
    )
    asked = lax.all_to_all(sent, "node", split_axis=0, concat_axis=0, tiled=True)
    place = lax.axis_index("local").reshape(1)
    answers = kernel_call(
        answer_kernel, (wide, LANES), BF16, [SMEM, VMEM] + [VMEM] * locals_, wide
    )(place, asked, *blocks)
    arrived = exchange(answers)
    grads = layer_call(wide)(
        history_lengths, owner, arrived, cotangent, w_in[0], w_out[0]
    )
    node_grads = exchange(grads)
    totals = kernel_call(total_kernel, (locals_ * rows_here, width), BF16, [VMEM, VMEM], wide)(
        asked, node_grads
    )
    totals = lax.all_to_all(
        totals.reshape(locals_, rows_here, width), "local", split_axis=0, concat_axis=0, tiled=True
    )
    return kernel_call(sum_kernel, (rows_here, width), BF16, [VMEM])(totals)


def solution(mesh):
    return jax.shard_map(
        per_device,
        mesh=mesh,
        in_specs=(
            P(("node", "local"), None),
            P(),
            P(),
            P(("node", "local"), None),
            P(("node", "local")),
            P(("node", "local"), None),
            P(("node", "local"), None),
        ),
        out_specs=P(("node", "local"), None),
        check_vma=False,
    )
```
